256 devices in a mesh: rows: 64 (over z, y, core), cols: 4 (over x).
Axes of the slice: x: 4, y: 4, z: 8, core: 2. Of those that a mesh axis runs over, the one named last changes fastest.
Arguments:
- hblocks: float32 [512, 24, 128, 128], P('rows'), may hold values from -0.0546875 to 0.0546875
- col_index: int32 [512, 24], P('rows'), may hold values from 0 to 511, as said below
- right_side: float32 [512, 64, 128], P('rows', 'cols'), may hold values from -12 to 12
- center: float32 [1], replicated, may hold values from -0.5 to 0.5
- shifts: float32 [8], replicated, may hold values from 0.05 to 2
- filter_weights: float32 [8], replicated, may hold values from 0.03 to 0.3
Outputs:
- filtered: float32 [512, 64, 128], P('rows', 'cols')
- gram_matrix: float32 [64, 64], P(None, 'cols')
- ritz_matrix: float32 [64, 64], P(None, 'cols')
The draws below stay inside these ranges and needn't reach their ends.
Inputs may be any that keep to these rules, and one draw needn't show every extreme that they name: `col_index`: block rows are held 8 to a device of rows, in order. In block row i the first 8 column indices are the 8 block rows of the device that holds i, each once. Every other column index of a block row lies on another device of rows; for each pair of distinct devices, the block rows of the one that are named by the block rows of the other are exactly 2 distinct ones.
All inputs are finite; a program needn't handle non-finite values.
Results may differ from the reference program's by a relative error of at most 0.0001.
Values sent between devices are 32-bit elements; how exact they have to be, the bound alone decides.
No kernel may reach another device: no remote copies, remote signals or barrier semaphores. Data moves between devices by JAX's collectives and lax.ppermute only.
A program may use at most 64 MiB of HBM per device.

```python
import math
import jax
import jax.numpy as jnp
from jax import lax

BLK = 128
NBLK = 24
NVEC = 64
POLES = 8
BR_DEV = 8
CAP = 2
ITERS = 2
NB = 512
N_ROWS = 64


def build_pattern(key):
    list_keys = jax.random.split(jax.random.fold_in(key, 7), N_ROWS * N_ROWS)
    shuffled = jax.vmap(lambda one_key: jax.random.permutation(one_key, BR_DEV))(list_keys)
    chosen = shuffled[:, :CAP].reshape(N_ROWS, N_ROWS, CAP).astype(jnp.int32)
    slot_total = (N_ROWS - 1) * CAP
    far_total = BR_DEV * (NBLK - BR_DEV)

    def one_device(device, device_key):
        extra_slots = jax.random.randint(jax.random.fold_in(device_key, 1), (far_total,), 0, slot_total, dtype=jnp.int32)
        counter = jnp.arange(far_total, dtype=jnp.int32)
        assigned = jnp.where(counter < slot_total, counter, extra_slots)
        assigned = jax.random.permutation(jax.random.fold_in(device_key, 2), assigned)
        owner_dev = assigned // CAP
        owner_dev = owner_dev + (owner_dev >= device).astype(jnp.int32)
        far_cols = owner_dev * BR_DEV + chosen[owner_dev, device, assigned % CAP]
        row_keys = jax.random.split(jax.random.fold_in(device_key, 3), BR_DEV)
        near_cols = jax.vmap(lambda one_key: jax.random.permutation(one_key, BR_DEV))(row_keys) + device * BR_DEV
        return jnp.concatenate([near_cols.astype(jnp.int32), far_cols.reshape(BR_DEV, NBLK - BR_DEV).astype(jnp.int32)], axis=1)
    device_keys = jax.random.split(jax.random.fold_in(key, 11), N_ROWS)
    columns = jax.vmap(one_device)(jnp.arange(N_ROWS, dtype=jnp.int32), device_keys)
    return columns.reshape(NB, NBLK)


def draw_col_index(key, part):
    return build_pattern(key)


def draw_right_side(key, part):
    position = jnp.arange(NB, dtype=jnp.float32)
    row_ramp = 1.0 + 2.0 * position / max(NB - 1, 1)
    row_rough = jnp.exp(jnp.log(2.0) * jax.random.uniform(jax.random.fold_in(key, 1), (NB, 1, 1)))
    col_rough = jnp.exp(jnp.log(2.0) * jax.random.uniform(jax.random.fold_in(key, 2), (1, NVEC, 1)))
    values = jax.random.normal(jax.random.fold_in(key, 3), (NB, NVEC, BLK))
    values = jnp.clip(values, -4.0, 4.0)
    return (values * row_ramp[:, None, None] * row_rough * col_rough / 4.0).astype(jnp.float32)


def block_levels(own_key, dims, cuts, smallest, top_value):
    def one(dim, blocks):
        heights = jax.random.uniform(jax.random.fold_in(jax.random.fold_in(own_key, 6), dim), (blocks,), jnp.float32, smallest / len(cuts), top_value / len(cuts))
        return jnp.repeat(jnp.exp(heights), dims[dim] // blocks).reshape((-1,) + (1,) * (len(dims) - dim - 1))

    loudness = one(*cuts[0])
    for cut in cuts[1:]:
        loudness = loudness * one(*cut)
    return loudness


def normal_values(rng, dims, spread, most, pieces=(), kind=jnp.bfloat16):
    values = jax.random.normal(rng, dims, jnp.float32) * spread
    if len(pieces) > 0:
        values = block_levels(rng, dims, pieces, -0.22, 0.18) * values
    return jnp.clip(values, min=-most, max=most).astype(kind)


def setup_inputs(seed: int = 0) -> dict:
    splits = jax.random.split(jax.random.key(seed), 7)
    return {
        "hblocks": normal_values(splits[0], (NB, NBLK, BLK, BLK), (4 * NBLK * BLK) ** -0.5, 0.0546875, ((0, 64),), jnp.float32),
        "col_index": draw_col_index(jax.random.fold_in(splits[6], 71), 0),
        "right_side": draw_right_side(jax.random.fold_in(splits[6], 71), 0),
        "center": jnp.clip(jax.random.uniform(splits[3], (1,), jnp.float32, -0.5, 0.5), -0.5, 0.5),
        "shifts": jnp.clip(jnp.exp(jax.random.uniform(splits[4], (POLES,), jnp.float32, math.log(0.05), math.log(2.0))), 0.05, 2.0),
        "filter_weights": jnp.clip(jnp.exp(jax.random.uniform(splits[5], (POLES,), jnp.float32, math.log(0.03), math.log(0.3))), 0.03, 0.3),
    }


exact_mode = lax.Precision.HIGHEST


def apply_h(vector, hblocks, col_index):
    gathered = vector[col_index]
    forward = jnp.einsum("ikab,ikvb->iva", hblocks, gathered, precision=exact_mode)
    transposed = jnp.einsum("ikab,iva->ikvb", hblocks, vector, precision=exact_mode)
    backward = jax.ops.segment_sum(transposed.reshape(-1, vector.shape[1], vector.shape[2]), col_index.reshape(-1), num_segments=vector.shape[0])
    return forward + backward


def column_dot(first_arr, second_arr):
    return jnp.sum(first_arr * second_arr, axis=(0, 2))


def reference(hblocks, col_index, right_side, center, shifts, filter_weights):
    center_value = center[0]
    base_shift = jnp.min(shifts)
    delta_shift = (shifts - base_shift)[:, None]

    def operate(vector):
        shifted = apply_h(vector, hblocks, col_index) - center_value * vector
        return apply_h(shifted, hblocks, col_index) - center_value * shifted + base_shift * vector

    residual = right_side
    direction = right_side
    solutions = jnp.zeros((POLES,) + right_side.shape, jnp.float32)
    shifted_dirs = jnp.broadcast_to(right_side, solutions.shape)
    res_norm = column_dot(residual, residual)
    zeta_prev = jnp.ones((POLES, NVEC), jnp.float32)
    zeta_now = jnp.ones((POLES, NVEC), jnp.float32)
    alpha_prev = jnp.ones((NVEC,), jnp.float32)
    beta_prev = jnp.zeros((NVEC,), jnp.float32)
    for iteration in range(ITERS):
        op_image = operate(direction)
        alpha_now = res_norm / column_dot(direction, op_image)
        zeta_next = zeta_now * zeta_prev * alpha_prev / (alpha_now * beta_prev * (zeta_prev - zeta_now) + zeta_prev * alpha_prev * (1.0 + delta_shift * alpha_now))
        zeta_ratio = zeta_next / zeta_now
        solutions = solutions + (alpha_now * zeta_ratio)[:, None, :, None] * shifted_dirs
        residual = residual - alpha_now[None, :, None] * op_image
        if iteration + 1 < ITERS:
            norm_next = column_dot(residual, residual)
            beta_now = norm_next / res_norm
            direction = residual + beta_now[None, :, None] * direction
            shifted_dirs = zeta_next[:, None, :, None] * residual[None] + (beta_now * zeta_ratio * zeta_ratio)[:, None, :, None] * shifted_dirs
            zeta_prev, zeta_now, alpha_prev, beta_prev, res_norm = zeta_now, zeta_next, alpha_now, beta_now, norm_next
    filtered = jnp.sum(filter_weights[:, None, None, None] * solutions, axis=0)
    applied = apply_h(filtered, hblocks, col_index)
    row_total = NB * BLK
    gram_matrix = jnp.einsum("iae,ibe->ab", filtered, filtered, precision=exact_mode) / row_total
    ritz_matrix = jnp.einsum("iae,ibe->ab", filtered, applied, precision=exact_mode) / row_total
    return filtered, gram_matrix, ritz_matrix
```

```python
import functools

import jax
import jax.numpy as jnp
from jax import lax
from jax.experimental import pallas as pl
from jax.experimental.pallas import tpu as pltpu
from jax.sharding import PartitionSpec as P

F32 = jnp.float32
BF16 = jnp.bfloat16
ROWS = 8
NEAR = 8
FAR = 16
VEC = 16
BLK = 128
PLANE = 8
DEPTH = 8
SLOTS = 16
TOTAL_ROWS = 65536.0

PLANE_GROUPS = [[z * PLANE + p for p in range(PLANE)] for z in range(DEPTH)]
DEPTH_GROUPS = [[z * PLANE + p for z in range(DEPTH)] for p in range(PLANE)]

PARAMS = pltpu.CompilerParams(vmem_limit_bytes=48 * 1024 * 1024)


def two_parts(x):
    high = x.astype(BF16)
    return high, (x - high.astype(F32)).astype(BF16)


def fold(d):
    return (d[:VEC, :BLK] + d[VEC:, BLK:]) + d[VEC:, :BLK] + d[:VEC, BLK:]


def times_block(vs, parts):
    return fold(jnp.dot(vs, jnp.concatenate(parts, axis=1), preferred_element_type=F32))


def times_block_t(vs, parts):
    return fold(
        lax.dot_general(
            vs,
            jnp.concatenate(parts, axis=0),
            (((1,), (1,)), ((), ())),
            preferred_element_type=F32,
        )
    )


def local_kernel(units, idx_ref, v_ref, h_ref, *refs):
    extras, send_ref, w_ref = refs[:-2], refs[-2], refs[-1]
    i = pl.program_id(0)

    @pl.when(i == 0)
    def _():
        w_ref[...] = jnp.zeros_like(w_ref)
        send_ref[...] = jnp.zeros_like(send_ref)
        for p in range(PLANE):
            send_ref[p * units + SLOTS] = extras[0][...]
            if len(extras) > 1:
                send_ref[p * units + SLOTS + 1] = extras[1][p]

    vs = jnp.concatenate(two_parts(v_ref[i]), axis=0)
    forward = jnp.zeros((VEC, BLK), F32)
    for k in range(NEAR + FAR):
        parts = two_parts(h_ref[0, k])
        t = times_block(vs, parts)
        where = idx_ref[i, k]
        if k < NEAR:
            w_ref[where] += t
            ns = jnp.concatenate(two_parts(v_ref[where]), axis=0)
            forward = forward + times_block_t(ns, parts)
        else:
            send_ref[where + (where >> 4) * (units - SLOTS)] += t
    w_ref[i] += forward


def middle_kernel(units, list_ref, recv_ref, zall_ref, zacc_ref, send_ref):
    zacc_ref[...] = jnp.zeros_like(zacc_ref)
    part = recv_ref[SLOTS]
    for p in range(1, PLANE):
        part = part + recv_ref[p * units + SLOTS]
    zacc_ref[DEPTH * ROWS] = part
    for p in range(PLANE):
        for s in range(SLOTS):
            row = (s // 2) * ROWS + list_ref[p, s]
            zacc_ref[row] += recv_ref[p * units + s]
            send_ref[p * SLOTS + s] = zall_ref[row]


def far_kernel(stage, idx_ref, z_ref, scal_ref, v_ref, w_ref, far_ref, zsum_ref, tot_ref, ha_ref, hb_ref, *refs):
    i = pl.program_id(0)
    center, base = scal_ref[0], scal_ref[1]
    acc = w_ref[i] + zsum_ref[i] - center * v_ref[i]
    for k in range(FAR):
        h = ha_ref[0, k] if k < FAR // 2 else hb_ref[0, k - FAR // 2]
        ns = jnp.concatenate(two_parts(far_ref[idx_ref[i, NEAR + k]]), axis=0)
        acc = acc + times_block_t(ns, two_parts(h))
    if stage == 1:
        zbuf_ref, out_ref, part_ref = refs
        square = acc * acc
    elif stage == 2:
        b_ref, rr_ref, zbuf_ref, out_ref, part_ref = refs
        rr = rr_ref[0]
        alpha = rr / (tot_ref[0] + base * rr)
        acc = b_ref[i] - alpha * (acc + base * b_ref[i])
        square = acc * acc
    else:
        b_ref, g_ref, rr_ref, out_ref, part_ref = refs
        beta = tot_ref[0] / rr_ref[0]
        direction = v_ref[i] + beta * b_ref[i]
        moved = acc + beta * g_ref[i]
        square = moved * moved + base * (direction * direction)
    out_ref[i] = acc
    if stage < 3:
        @pl.when(i == 0)
        def _():
            zbuf_ref[...] = jnp.zeros_like(zbuf_ref)
        zbuf_ref[z_ref[0] * ROWS + i] = acc

    @pl.when(i == 0)
    def _():
        part_ref[...] = square

    @pl.when(i > 0)
    def _():
        part_ref[...] += square

    @pl.when(i == ROWS - 1)
    def _():
        part_ref[...] = jnp.broadcast_to(jnp.sum(part_ref[...], axis=1, keepdims=True), (VEC, BLK))


def whole(shape):
    return pl.BlockSpec(shape, lambda *_: (0,) * len(shape))


def local_products(units, idx, v, h, extras):
    return pl.pallas_call(
        functools.partial(local_kernel, units),
        grid_spec=pltpu.PrefetchScalarGridSpec(
            num_scalar_prefetch=1,
            grid=(ROWS,),
            in_specs=[
                whole((ROWS, VEC, BLK)),
                pl.BlockSpec((1, NEAR + FAR, BLK, BLK), lambda i, *_: (i, 0, 0, 0)),
            ]
            + [whole(e.shape) for e in extras],
            out_specs=[whole((PLANE * units, VEC, BLK)), whole((ROWS, VEC, BLK))],
        ),
        out_shape=[
            jax.ShapeDtypeStruct((PLANE * units, VEC, BLK), F32),
            jax.ShapeDtypeStruct((ROWS, VEC, BLK), F32),
        ],
        compiler_params=PARAMS,
        name="local_products",
    )(idx, v, h, *extras)


def middle(units, lists, recv, zall):
    return pl.pallas_call(
        functools.partial(middle_kernel, units),
        grid_spec=pltpu.PrefetchScalarGridSpec(
            num_scalar_prefetch=1,
            grid=(1,),
            in_specs=[whole((PLANE * units, VEC, BLK)), whole((DEPTH * ROWS, VEC, BLK))],
            out_specs=[
                whole((DEPTH * ROWS + 1, VEC, BLK)),
                whole((PLANE * SLOTS, VEC, BLK)),
            ],
        ),
        out_shape=[
            jax.ShapeDtypeStruct((DEPTH * ROWS + 1, VEC, BLK), F32),
            jax.ShapeDtypeStruct((PLANE * SLOTS, VEC, BLK), F32),
        ],
        compiler_params=PARAMS,
        name="middle",
    )(lists, recv, zall)


def far_products(stage, idx, my_z, scalars, v, w, far, zsum, h, *more):
    unit = pl.BlockSpec((1, VEC, BLK), lambda *_: (DEPTH * ROWS, 0, 0))
    vec = whole((ROWS, VEC, BLK))
    half = FAR // 2
    extra_specs = {1: [], 2: [vec, unit], 3: [vec, vec, unit]}[stage]
    out_specs = [vec, whole((VEC, BLK))]
    out_shape = [
        jax.ShapeDtypeStruct((ROWS, VEC, BLK), F32),
        jax.ShapeDtypeStruct((VEC, BLK), F32),
    ]
    if stage < 3:
        out_specs = [whole((DEPTH * ROWS, VEC, BLK))] + out_specs
        out_shape = [jax.ShapeDtypeStruct((DEPTH * ROWS, VEC, BLK), F32)] + out_shape
    return pl.pallas_call(
        functools.partial(far_kernel, stage),
        grid_spec=pltpu.PrefetchScalarGridSpec(
            num_scalar_prefetch=3,
            grid=(ROWS,),
            in_specs=[
                vec,
                vec,
                whole((PLANE * SLOTS, VEC, BLK)),
                pl.BlockSpec((ROWS, VEC, BLK), lambda i, idx, z, s: (z[0], 0, 0)),
                unit,
                pl.BlockSpec((1, half, BLK, BLK), lambda i, *_: (i, 1, 0, 0)),
                pl.BlockSpec((1, half, BLK, BLK), lambda i, *_: (i, 2, 0, 0)),
            ]
            + extra_specs,
            out_specs=out_specs,
        ),
        out_shape=out_shape,
        compiler_params=PARAMS,
        name="far_products",
    )(idx, my_z, scalars, v, w, far, zsum, zsum, h, h, *more)


def gram_kernel(all_ref, b_ref, r_ref, g_ref, gr_ref, out_ref):
    total = jnp.zeros((2 * 4 * VEC, 4 * VEC), F32)
    for i in range(ROWS):
        left = jnp.concatenate([all_ref[0, i], all_ref[1, i]], axis=0)
        right = jnp.concatenate([b_ref[i], r_ref[i], g_ref[i], gr_ref[i]], axis=0)
        total = total + lax.dot_general(
            left,
            right,
            (((1,), (1,)), ((), ())),
            precision=lax.Precision.HIGHEST,
            preferred_element_type=F32,
        )
    out_ref[...] = total


def shards(hblocks, col_index, right_side, center, shifts, filter_weights):
    device = lax.axis_index("rows").astype(jnp.int32)
    my_z = (device // PLANE).reshape(1)
    own_cols = col_index[:, :NEAR] - device * ROWS
    far_cols = col_index[:, NEAR:]
    flat = far_cols.reshape(-1)
    owner = flat // ROWS
    smaller = (owner[:, None] == owner[None, :]) & (flat[None, :] < flat[:, None])
    slot = jnp.any(smaller, axis=1).astype(jnp.int32)
    flat_slot = (owner % PLANE) * SLOTS + (owner // PLANE) * 2 + slot
    idx = jnp.concatenate([own_cols, flat_slot.reshape(ROWS, FAR)], axis=1)
    named = flat_slot[None, :] == jnp.arange(PLANE * SLOTS, dtype=jnp.int32)[:, None]
    lists = jnp.max(jnp.where(named, (flat % ROWS)[None, :], 0), axis=1)
    lists_out = jnp.pad(
        lists.astype(F32).reshape(PLANE, 1, SLOTS), ((0, 0), (0, VEC - 1), (0, BLK - SLOTS))
    )

    base_shift = jnp.min(shifts)
    scalars = jnp.stack([center[0], base_shift])
    b = right_side
    part = jnp.broadcast_to(jnp.sum(b * b, axis=(0, 2))[:, None], (VEC, BLK))
    zbuf = lax.dynamic_update_slice(
        jnp.zeros((DEPTH * ROWS, VEC, BLK), F32), b, (my_z[0] * ROWS, 0, 0)
    )

    def plane_exchange(x):
        return lax.all_to_all(
            x, "rows", split_axis=0, concat_axis=0, tiled=True, axis_index_groups=PLANE_GROUPS
        )

    def depth_sum(x):
        return lax.psum(x, "rows", axis_index_groups=DEPTH_GROUPS)

    units = SLOTS + 2
    send, w = local_products(units, idx, b, hblocks, [part, lists_out])
    recv = plane_exchange(send)
    zall = depth_sum(zbuf)
    peer_lists = recv.reshape(PLANE, units, VEC, BLK)[:, SLOTS + 1, 0, :SLOTS].astype(jnp.int32)
    zacc, send = middle(units, peer_lists, recv, zall)
    far = plane_exchange(send)
    zsum1 = depth_sum(zacc)
    zbuf, g0, part = far_products(1, idx, my_z, scalars, b, w, far, zsum1, hblocks)

    units = SLOTS + 1
    send, w = local_products(units, idx, g0, hblocks, [part])
    recv = plane_exchange(send)
    zall = depth_sum(zbuf)
    zacc, send = middle(units, peer_lists, recv, zall)
    far = plane_exchange(send)
    zsum2 = depth_sum(zacc)
    zbuf, r1, part = far_products(2, idx, my_z, scalars, g0, w, far, zsum2, hblocks, b, zsum1)

    send, w = local_products(units, idx, r1, hblocks, [part])
    recv = plane_exchange(send)
    zall = depth_sum(zbuf)
    zacc, send = middle(units, peer_lists, recv, zall)
    far = plane_exchange(send)
    zsum3 = depth_sum(zacc)
    gr, part = far_products(3, idx, my_z, scalars, r1, w, far, zsum3, hblocks, b, g0, zsum1)

    both = lax.all_gather(jnp.stack([b, r1]), "cols", axis=2, tiled=True)
    gram = pl.pallas_call(
        gram_kernel,
        out_shape=jax.ShapeDtypeStruct((8 * VEC, 4 * VEC), F32),
        compiler_params=PARAMS,
        name="gram",
    )(both, b, r1, g0, gr)
    packed = jnp.concatenate([jnp.pad(gram, ((0, 0), (0, BLK - 4 * VEC))), part], axis=0)
    packed = lax.psum(packed, "rows", axis_index_groups=DEPTH_GROUPS)
    packed = lax.psum(packed, "rows", axis_index_groups=PLANE_GROUPS)

    rr0 = zsum1[DEPTH * ROWS, :, 0]
    d0 = zsum2[DEPTH * ROWS, :, 0] + base_shift * rr0
    rr1 = zsum3[DEPTH * ROWS, :, 0]
    d1 = packed[8 * VEC :, 0]
    alpha0 = rr0 / d0
    beta = rr1 / rr0
    alpha1 = rr1 / d1
    delta = (shifts - base_shift)[:, None]
    zeta1 = 1.0 / (1.0 + delta * alpha0)
    zeta2 = zeta1 * alpha0 / (alpha1 * beta * (1.0 - zeta1) + alpha0 * (1.0 + delta * alpha1))
    weights = filter_weights[:, None]
    coef_b = jnp.sum(weights * (alpha0 * zeta1 + alpha1 * beta * zeta1 * zeta2), axis=0)
    coef_r = jnp.sum(weights * (alpha1 * zeta2), axis=0)
    filtered = coef_b[None, :, None] * b + coef_r[None, :, None] * r1
    all_coef = lax.all_gather(jnp.stack([coef_b, coef_r]), "cols", axis=1, tiled=True)
    left_b, left_r = all_coef[0][:, None], all_coef[1][:, None]
    top, low = packed[: 4 * VEC], packed[4 * VEC : 8 * VEC]
    mixed = left_b * top + left_r * low
    n = VEC
    gram_matrix = mixed[:, :n] * coef_b + mixed[:, n : 2 * n] * coef_r
    ritz = mixed[:, 2 * n : 3 * n] * coef_b + mixed[:, 3 * n : 4 * n] * coef_r
    ritz = ritz + center[0] * gram_matrix
    return filtered, gram_matrix / TOTAL_ROWS, ritz / TOTAL_ROWS


def solution(mesh):
    placed = (P("rows", None, None, None), P("rows", None), P("rows", "cols", None), P(), P(), P())
    return jax.shard_map(
        shards,
        mesh=mesh,
        in_specs=placed,
        out_specs=(P("rows", "cols", None), P(None, "cols"), P(None, "cols")),
        check_vma=False,
    )
```

```python
import functools

import jax
import jax.numpy as jnp
from jax import lax
from jax.experimental import pallas as pl
from jax.experimental.pallas import tpu as pltpu
from jax.sharding import PartitionSpec as P

F32 = jnp.float32
BF16 = jnp.bfloat16
ROWS = 8
NEAR = 8
FAR = 16
VEC = 16
BLK = 128
PEERS = 64
PLANE = 8
DEPTH = 8
NY = 4
NX = 4
SLOTS = 16
UNITS = ROWS + 1
TOTAL_ROWS = 65536.0

DEPTH_GROUPS = [[z * PLANE + p for z in range(DEPTH)] for p in range(PLANE)]

IN_VMEM = pl.BlockSpec(memory_space=pltpu.VMEM)
IN_SMEM = pl.BlockSpec(memory_space=pltpu.SMEM)
IN_ANY = pl.BlockSpec(memory_space=pl.ANY)


def params(mib):
    return pltpu.CompilerParams(vmem_limit_bytes=mib * 1024 * 1024)


def shape(*dims):
    return jax.ShapeDtypeStruct(dims, F32)


def peer_number(k, p):
    return ((p // 2 + k // 2) % NY) * 2 + (p % 2 + k % 2) % 2


def plane_shift(k):
    return [
        (z * PLANE + p, z * PLANE + peer_number(k, p)) for z in range(DEPTH) for p in range(PLANE)
    ]


def depth_shift(k):
    return [(d, (d + k * PLANE) % PEERS) for d in range(PEERS)]


def two_parts(x):
    high = x.astype(BF16)
    return high, (x - high.astype(F32)).astype(BF16)


def stacked(x):
    return jnp.concatenate(two_parts(x), axis=0)


def fold(d):
    return (d[:VEC, :BLK] + d[VEC:, BLK:]) + d[VEC:, :BLK] + d[:VEC, BLK:]


def times_block(vs, high, low):
    return fold(jnp.dot(vs, jnp.concatenate([high, low], axis=1), preferred_element_type=F32))


def times_blocks_t(ns, blocks):
    weights = jnp.concatenate(
        [jnp.concatenate([b[part] for b in blocks], axis=1) for part in range(2)], axis=0
    )
    return fold(
        lax.dot_general(
            jnp.concatenate(ns, axis=1),
            weights,
            (((1,), (1,)), ((), ())),
            preferred_element_type=F32,
        )
    )


def column_sums(x):
    return jnp.broadcast_to(jnp.sum(x, axis=1, keepdims=True), (VEC, BLK))


def start_copies(h_ref, first, buffer, sems):
    count = buffer.shape[1]
    for i in range(ROWS):
        pltpu.make_async_copy(
            h_ref.at[i, pl.ds(first, count)], buffer.at[i], sems.at[i]
        ).start()


def wait_copy(h_ref, first, buffer, sems, i):
    count = buffer.shape[1]
    pltpu.make_async_copy(h_ref.at[i, pl.ds(first, count)], buffer.at[i], sems.at[i]).wait()


def far_kernel(first, place_ref, my_ref, v_ref, more_ref, h_ref, *refs):
    outs, (acc_ref, buffer, sems) = refs[:PLANE], refs[PLANE:]
    start_copies(h_ref, NEAR, buffer, sems)
    acc_ref[...] = jnp.zeros_like(acc_ref)
    if first:
        part = jnp.zeros((VEC, BLK), F32)
        for i in range(ROWS):
            part = part + v_ref[i] * v_ref[i]
        part = column_sums(part)
        for k in range(PLANE):
            outs[k][SLOTS + 1] = more_ref[peer_number(k, my_ref[1])]
    else:
        part = more_ref[...]

    def body(i, carry):
        vs = stacked(v_ref[i])
        wait_copy(h_ref, NEAR, buffer, sems, i)
        for k in range(FAR):
            acc_ref[place_ref[i, k]] += times_block(vs, *two_parts(buffer[i, k]))
        return carry

    lax.fori_loop(0, ROWS, body, 0)
    for k in range(PLANE):
        outs[k][:SLOTS] = acc_ref[k * SLOTS : (k + 1) * SLOTS]
        outs[k][SLOTS] = part


def near_kernel(own_ref, v_ref, h_ref, w_ref, parts, buffer, sems):
    start_copies(h_ref, 0, buffer, sems)
    for i in range(ROWS):
        parts[i] = stacked(v_ref[i])
    w_ref[...] = jnp.zeros_like(w_ref)

    def body(i, carry):
        vs = parts[i]
        acc = jnp.zeros((VEC, BLK), F32)
        wait_copy(h_ref, 0, buffer, sems, i)
        for k in range(0, NEAR, 2):
            blocks = [two_parts(buffer[i, q]) for q in (k, k + 1)]
            acc = acc + times_blocks_t(
                [parts[own_ref[i, k]], parts[own_ref[i, k + 1]]], blocks
            )
            for q in range(2):
                w_ref[own_ref[i, k + q]] += times_block(vs, *blocks[q])
        w_ref[i] += acc
        return carry

    lax.fori_loop(0, ROWS, body, 0)


def middle_kernel(list_ref, zv_ref, *refs):
    recvs, outs, zacc_ref = refs[:PLANE], refs[PLANE:-1], refs[-1]
    for k in range(PLANE):
        back = ((NY - k // 2) % NY) * 2 + k % 2
        for s in range(SLOTS):
            outs[k][s] = zv_ref[(s // 2) * ROWS + list_ref[back, s]]
    zacc_ref[...] = jnp.zeros_like(zacc_ref)
    part = recvs[0][SLOTS]
    for k in range(1, PLANE):
        part = part + recvs[k][SLOTS]
    for z in range(DEPTH):
        zacc_ref[z * UNITS + ROWS] = part
    for s in range(SLOTS):
        for k in range(PLANE):
            zacc_ref[(s // 2) * UNITS + list_ref[k, s]] += recvs[k][s]


def finish_kernel(stage, place_ref, scal_ref, v_ref, w_ref, rz_ref, h_ref, *refs):
    fars, refs = refs[:PLANE], refs[PLANE:]
    refs, (parts, buffer, sems) = refs[:-3], refs[-3:]
    start_copies(h_ref, NEAR, buffer, sems)
    center, base = scal_ref[0], scal_ref[1]
    total = rz_ref[ROWS]
    for z in range(1, DEPTH):
        total = total + rz_ref[z * UNITS + ROWS]
    for k in range(PLANE):
        for s in range(SLOTS):
            parts[k * SLOTS + s] = stacked(fars[k][s])
    if stage == 1:
        out_ref, part_ref, tot_ref = refs
    elif stage == 2:
        b_ref, rr_ref, out_ref, part_ref, tot_ref, br_ref = refs
        rr = rr_ref[...]
        alpha = rr / (total + base * rr)
    else:
        b_ref, g_ref, rr_ref, out_ref, part_ref, tot_ref = refs
        beta = total / rr_ref[...]
    tot_ref[...] = total

    def body(i, square):
        acc = w_ref[i] - center * v_ref[i]
        for z in range(DEPTH):
            acc = acc + rz_ref[z * UNITS + i]
        wait_copy(h_ref, NEAR, buffer, sems, i)
        for k in range(0, FAR, 4):
            ks = range(k, k + 4)
            acc = acc + times_blocks_t(
                [parts[place_ref[i, q]] for q in ks], [two_parts(buffer[i, q]) for q in ks]
            )
        if stage == 1:
            new = acc * acc
        elif stage == 2:
            acc = b_ref[i] - alpha * (acc + base * b_ref[i])
            br_ref[i] = b_ref[i]
            br_ref[ROWS + i] = acc
            new = acc * acc
        else:
            direction = v_ref[i] + beta * b_ref[i]
            moved = acc + beta * g_ref[i]
            new = moved * moved + base * (direction * direction)
        if stage == 3:
            out_ref[i] = acc
        else:
            for z in range(DEPTH):
                out_ref[z * ROWS + i] = acc
        return square + new

    square = lax.fori_loop(0, ROWS, body, jnp.zeros((VEC, BLK), F32))
    part_ref[...] = column_sums(square)


def gram_kernel(x_ref, g_ref, gr_ref, part_ref, *refs):
    lefts, out_ref = refs[:NX], refs[NX]
    own = lefts[0]
    total = jnp.zeros((2 * NX * VEC, 4 * VEC), F32)
    for i in range(ROWS):
        left = jnp.concatenate(
            [lefts[k][i] for k in range(NX)] + [lefts[k][ROWS + i] for k in range(NX)], axis=0
        )
        right = jnp.concatenate([own[i], own[ROWS + i], g_ref[i], gr_ref[i]], axis=0)
        total = total + lax.dot_general(
            left,
            right,
            (((1,), (1,)), ((), ())),
            precision=lax.Precision.HIGHEST,
            preferred_element_type=F32,
        )
    both = jnp.concatenate([total[: NX * VEC], total[NX * VEC :]], axis=1)
    for k in range(NX):
        start = pl.multiple_of(((x_ref[0] + NX - k) % NX) * VEC, VEC)
        out_ref[pl.ds(start, VEC), :] = both[k * VEC : (k + 1) * VEC]
    out_ref[NX * VEC :, :] = part_ref[...]


def sum_kernel(*refs):
    total = refs[0][...]
    for ref in refs[1:-1]:
        total = total + ref[...]
    refs[-1][...] = total


def add_up(x, shifts):
    every = [x] + [lax.ppermute(x, "rows", shift) for shift in shifts]
    return pl.pallas_call(
        sum_kernel,
        in_specs=[IN_VMEM] * len(every),
        out_specs=IN_VMEM,
        out_shape=shape(*x.shape),
        compiler_params=params(4),
        name="sum",
    )(*every)


def shards(hblocks, col_index, right_side, center, shifts, filter_weights):
    device = lax.axis_index("rows").astype(jnp.int32)
    my_z, my_p = device // PLANE, device % PLANE
    my = jnp.stack([my_z, my_p])
    own_cols = col_index[:, :NEAR] - device * ROWS
    flat = col_index[:, NEAR:].reshape(-1)
    owner = flat // ROWS
    smaller = (owner[:, None] == owner[None, :]) & (flat[None, :] < flat[:, None])
    slot = (owner // PLANE) * 2 + jnp.any(smaller, axis=1).astype(jnp.int32)
    owner_p = owner % PLANE
    there = ((owner_p // 2 + NY - my_p // 2) % NY) * 2 + (my_p + owner_p) % 2
    back = ((my_p // 2 + NY - owner_p // 2) % NY) * 2 + (my_p + owner_p) % 2
    to_place = (there * SLOTS + slot).reshape(ROWS, FAR)
    from_place = (back * SLOTS + slot).reshape(ROWS, FAR)
    flat_slot = owner_p * SLOTS + slot
    named = flat_slot[None, :] == jnp.arange(PLANE * SLOTS, dtype=jnp.int32)[:, None]
    lists = jnp.max(jnp.where(named, (flat % ROWS)[None, :], 0), axis=1)
    lists_out = jnp.pad(
        lists.astype(F32).reshape(PLANE, 1, SLOTS), ((0, 0), (0, VEC - 1), (0, BLK - SLOTS))
    )

    base_shift = jnp.min(shifts)
    scalars = jnp.stack([center[0], base_shift])
    b = right_side
    h = pltpu.with_memory_space_constraint(hblocks, pltpu.HBM)
    sems = pltpu.SemaphoreType.DMA((ROWS,))
    far_buffer = pltpu.VMEM((ROWS, FAR, BLK, BLK), F32)

    def plane_exchange(xs):
        return [xs[0]] + [lax.ppermute(xs[k], "rows", plane_shift(k)) for k in range(1, PLANE)]

    def depth_exchange(x):
        return lax.all_to_all(
            x, "rows", split_axis=0, concat_axis=0, tiled=True, axis_index_groups=DEPTH_GROUPS
        )

    def far_products(first, v, more):
        return pl.pallas_call(
            functools.partial(far_kernel, first),
            in_specs=[IN_SMEM] * 2 + [IN_VMEM] * 2 + [IN_ANY],
            out_specs=[IN_VMEM] * PLANE,
            out_shape=[shape(SLOTS + (2 if first else 1), VEC, BLK)] * PLANE,
            scratch_shapes=[pltpu.VMEM((PLANE * SLOTS, VEC, BLK), F32), far_buffer, sems],
            compiler_params=params(20),
            name="far",
        )(to_place, my, v, more, h)

    def near_products(v):
        return pl.pallas_call(
            near_kernel,
            in_specs=[IN_SMEM, IN_VMEM, IN_ANY],
            out_specs=IN_VMEM,
            out_shape=shape(ROWS, VEC, BLK),
            scratch_shapes=[
                pltpu.VMEM((ROWS, 2 * VEC, BLK), BF16),
                pltpu.VMEM((ROWS, NEAR, BLK, BLK), F32),
                sems,
            ],
            compiler_params=params(12),
            name="near",
        )(own_cols, v, h)

    def apply(stage, lists, v, zv, recvs, *more):
        outs = pl.pallas_call(
            middle_kernel,
            in_specs=[IN_SMEM] + [IN_VMEM] * (PLANE + 1),
            out_specs=[IN_VMEM] * (PLANE + 1),
            out_shape=[shape(SLOTS, VEC, BLK)] * PLANE + [shape(DEPTH * UNITS, VEC, BLK)],
            compiler_params=params(12),
            name="middle",
        )(lists, zv, *recvs)
        rz = depth_exchange(outs[PLANE])
        fars = plane_exchange(outs[:PLANE])
        w = near_products(v)
        outs = [shape(ROWS * (DEPTH if stage < 3 else 1), VEC, BLK)] + [shape(VEC, BLK)] * 2
        if stage == 2:
            outs.append(shape(2 * ROWS, VEC, BLK))
        return pl.pallas_call(
            functools.partial(finish_kernel, stage),
            in_specs=[IN_SMEM] * 2
            + [IN_VMEM] * 3
            + [IN_ANY]
            + [IN_VMEM] * (PLANE + len(more)),
            out_specs=[IN_VMEM] * len(outs),
            out_shape=outs,
            scratch_shapes=[
                pltpu.VMEM((PLANE * SLOTS, 2 * VEC, BLK), BF16),
                far_buffer,
                sems,
            ],
            compiler_params=params(20),
            name="finish",
        )(from_place, scalars, v, w, rz, h, *fars, *more)

    zv = depth_exchange(jnp.tile(b, (DEPTH, 1, 1)))
    recvs = plane_exchange(far_products(True, b, lists_out))
    peer_lists = jnp.stack([r[SLOTS + 1, 0, :SLOTS] for r in recvs]).astype(jnp.int32)
    g0, part, rr0 = apply(1, peer_lists, b, zv, recvs)

    zv = depth_exchange(g0)
    recvs = plane_exchange(far_products(False, g0, part))
    r1, part, moved0, br = apply(2, peer_lists, g0, zv, recvs, b, rr0)

    zv = depth_exchange(r1)
    recvs = plane_exchange(far_products(False, r1, part))
    lefts = [br] + [
        lax.ppermute(br, "cols", [(x, (x + k) % NX) for x in range(NX)]) for k in range(1, NX)
    ]
    gr, part, rr1 = apply(3, peer_lists, r1, zv, recvs, b, g0, rr0)

    my_x = lax.axis_index("cols").astype(jnp.int32).reshape(1)
    packed = pl.pallas_call(
        gram_kernel,
        in_specs=[IN_SMEM] + [IN_VMEM] * (3 + NX),
        out_specs=IN_VMEM,
        out_shape=shape((NX + 1) * VEC, BLK),
        compiler_params=params(8),
        name="gram",
    )(my_x, g0, gr, part, *lefts)
    packed = add_up(packed, [plane_shift(k) for k in range(1, PLANE)])
    packed = add_up(packed, [depth_shift(k) for k in range(1, DEPTH)])

    rr0 = rr0[:, 0]
    d0 = moved0[:, 0] + base_shift * rr0
    rr1 = rr1[:, 0]
    d1 = packed[NX * VEC :, 0]
    alpha0 = rr0 / d0
    beta = rr1 / rr0
    alpha1 = rr1 / d1
    delta = (shifts - base_shift)[:, None]
    zeta1 = 1.0 / (1.0 + delta * alpha0)
    zeta2 = zeta1 * alpha0 / (alpha1 * beta * (1.0 - zeta1) + alpha0 * (1.0 + delta * alpha1))
    weights = filter_weights[:, None]
    coef_b = jnp.sum(weights * (alpha0 * zeta1 + alpha1 * beta * zeta1 * zeta2), axis=0)
    coef_r = jnp.sum(weights * (alpha1 * zeta2), axis=0)
    filtered = coef_b[None, :, None] * b + coef_r[None, :, None] * r1[:ROWS]
    all_coef = lax.all_gather(jnp.stack([coef_b, coef_r]), "cols", axis=1, tiled=True)
    left_b, left_r = all_coef[0][:, None], all_coef[1][:, None]
    n = VEC
    mixed = left_b * packed[: NX * n, : 4 * n] + left_r * packed[: NX * n, 4 * n :]
    gram_matrix = mixed[:, :n] * coef_b + mixed[:, n : 2 * n] * coef_r
    ritz = mixed[:, 2 * n : 3 * n] * coef_b + mixed[:, 3 * n :] * coef_r
    ritz = ritz + center[0] * gram_matrix
    return filtered, gram_matrix / TOTAL_ROWS, ritz / TOTAL_ROWS


def solution(mesh):
    placed = (P("rows", None, None, None), P("rows", None), P("rows", "cols", None), P(), P(), P())
    return jax.shard_map(
        shards,
        mesh=mesh,
        in_specs=placed,
        out_specs=(P("rows", "cols", None), P(None, "cols"), P(None, "cols")),
        check_vma=False,
    )
```

```python
import functools

import jax
import jax.numpy as jnp
from jax import lax
from jax.experimental import pallas as pl
from jax.experimental.pallas import tpu as pltpu
from jax.sharding import PartitionSpec as P

F32 = jnp.float32
BF16 = jnp.bfloat16
ROWS = 8
NEAR = 8
FAR = 16
VEC = 16
BLK = 128
PEERS = 64
PLANE = 8
DEPTH = 8
NY = 4
NX = 4
SLOTS = 16
UNITS = ROWS + 1
TOTAL_ROWS = 65536.0

DEPTH_GROUPS = [[z * PLANE + p for z in range(DEPTH)] for p in range(PLANE)]

IN_VMEM = pl.BlockSpec(memory_space=pltpu.VMEM)
IN_SMEM = pl.BlockSpec(memory_space=pltpu.SMEM)
IN_ANY = pl.BlockSpec(memory_space=pl.ANY)


def params(mib):
    return pltpu.CompilerParams(vmem_limit_bytes=mib * 1024 * 1024)


def cost(us):
    return pl.CostEstimate(flops=int(us * 1e9), bytes_accessed=int(us * 3.2e6), transcendentals=0)


def shape(*dims):
    return jax.ShapeDtypeStruct(dims, F32)


def peer_number(k, p):
    return ((p // 2 + k // 2) % NY) * 2 + (p % 2 + k % 2) % 2


def plane_shift(k):
    return [
        (z * PLANE + p, z * PLANE + peer_number(k, p)) for z in range(DEPTH) for p in range(PLANE)
    ]


def column_shift(k):
    return [(x, (x + k) % NX) for x in range(NX)]


def two_parts(x):
    high = x.astype(BF16)
    return high, (x - high.astype(F32)).astype(BF16)


def stacked(x):
    return jnp.concatenate(two_parts(x), axis=0)


def fold(d):
    return (d[:VEC, :BLK] + d[VEC:, BLK:]) + d[VEC:, :BLK] + d[:VEC, BLK:]


def times_block(vs, high, low):
    return fold(jnp.dot(vs, jnp.concatenate([high, low], axis=1), preferred_element_type=F32))


def times_blocks_t(ns, blocks):
    weights = jnp.concatenate(
        [jnp.concatenate([b[part] for b in blocks], axis=1) for part in range(2)], axis=0
    )
    return fold(
        lax.dot_general(
            jnp.concatenate(ns, axis=1),
            weights,
            (((1,), (1,)), ((), ())),
            preferred_element_type=F32,
        )
    )


def column_sums(x):
    return jnp.broadcast_to(jnp.sum(x, axis=1, keepdims=True), (VEC, BLK))


def start_copies(h_ref, first, buffer, sems):
    count = buffer.shape[1]
    for i in range(ROWS):
        pltpu.make_async_copy(
            h_ref.at[i, pl.ds(first, count)], buffer.at[i], sems.at[i]
        ).start()


def wait_copy(h_ref, first, buffer, sems, i):
    count = buffer.shape[1]
    pltpu.make_async_copy(h_ref.at[i, pl.ds(first, count)], buffer.at[i], sems.at[i]).wait()


def far_kernel(first, place_ref, my_ref, v_ref, more_ref, h_ref, *refs):
    outs, (acc_ref, buffer, sems) = refs[:PLANE], refs[PLANE:]
    start_copies(h_ref, NEAR, buffer, sems)
    acc_ref[...] = jnp.zeros_like(acc_ref)
    if first:
        part = jnp.zeros((VEC, BLK), F32)
        for i in range(ROWS):
            part = part + v_ref[i] * v_ref[i]
        part = column_sums(part)
        for k in range(PLANE):
            outs[k][SLOTS + 1] = more_ref[peer_number(k, my_ref[1])]
    else:
        part = more_ref[...]

    def body(i, carry):
        vs = stacked(v_ref[i])
        wait_copy(h_ref, NEAR, buffer, sems, i)
        for k in range(FAR):
            acc_ref[place_ref[i, k]] += times_block(vs, *two_parts(buffer[i, k]))
        return carry

    lax.fori_loop(0, ROWS, body, 0)
    for k in range(PLANE):
        outs[k][:SLOTS] = acc_ref[k * SLOTS : (k + 1) * SLOTS]
        outs[k][SLOTS] = part


def near_kernel(own_ref, v_ref, h_ref, w_ref, parts, buffer, sems):
    start_copies(h_ref, 0, buffer, sems)
    for i in range(ROWS):
        parts[i] = stacked(v_ref[i])
    w_ref[...] = jnp.zeros_like(w_ref)

    def body(i, carry):
        vs = parts[i]
        acc = jnp.zeros((VEC, BLK), F32)
        wait_copy(h_ref, 0, buffer, sems, i)
        for k in range(0, NEAR, 2):
            blocks = [two_parts(buffer[i, q]) for q in (k, k + 1)]
            acc = acc + times_blocks_t(
                [parts[own_ref[i, k]], parts[own_ref[i, k + 1]]], blocks
            )
            for q in range(2):
                w_ref[own_ref[i, k + q]] += times_block(vs, *blocks[q])
        w_ref[i] += acc
        return carry

    lax.fori_loop(0, ROWS, body, 0)


def middle_kernel(list_ref, zv_ref, *refs):
    recvs, outs, zacc_ref = refs[:PLANE], refs[-PLANE - 1 : -1], refs[-1]
    for k in range(PLANE):
        back = ((NY - k // 2) % NY) * 2 + k % 2
        for s in range(SLOTS):
            outs[k][s] = zv_ref[(s // 2) * ROWS + list_ref[back, s]]
    zacc_ref[...] = jnp.zeros_like(zacc_ref)
    part = recvs[0][SLOTS]
    for k in range(1, PLANE):
        part = part + recvs[k][SLOTS]
    for z in range(DEPTH):
        zacc_ref[z * UNITS + ROWS] = part
    for s in range(SLOTS):
        for k in range(PLANE):
            zacc_ref[(s // 2) * UNITS + list_ref[k, s]] += recvs[k][s]


def finish_kernel(stage, place_ref, scal_ref, v_ref, w_ref, rz_ref, h_ref, *refs):
    fars, refs = refs[:PLANE], refs[PLANE:]
    refs, (parts, buffer, sems) = refs[:-3], refs[-3:]
    start_copies(h_ref, NEAR, buffer, sems)
    center, base = scal_ref[0], scal_ref[1]
    total = rz_ref[ROWS]
    for z in range(1, DEPTH):
        total = total + rz_ref[z * UNITS + ROWS]
    for k in range(PLANE):
        for s in range(SLOTS):
            parts[k * SLOTS + s] = stacked(fars[k][s])
    if stage == 1:
        all_ref, part_ref, tot_ref, out_ref = refs
    elif stage == 2:
        b_ref, rr_ref, all_ref, part_ref, tot_ref, out_ref, br_ref = refs
        rr = rr_ref[...]
        alpha = rr / (total + base * rr)
    else:
        b_ref, g_ref, rr_ref, out_ref, part_ref, tot_ref = refs
        beta = total / rr_ref[...]
    tot_ref[...] = total

    def body(i, square):
        acc = w_ref[i] - center * v_ref[i]
        for z in range(DEPTH):
            acc = acc + rz_ref[z * UNITS + i]
        wait_copy(h_ref, NEAR, buffer, sems, i)
        for k in range(0, FAR, 4):
            ks = range(k, k + 4)
            acc = acc + times_blocks_t(
                [parts[place_ref[i, q]] for q in ks], [two_parts(buffer[i, q]) for q in ks]
            )
        if stage == 1:
            new = acc * acc
        elif stage == 2:
            acc = b_ref[i] - alpha * (acc + base * b_ref[i])
            br_ref[i] = b_ref[i]
            br_ref[ROWS + i] = acc
            new = acc * acc
        else:
            direction = v_ref[i] + beta * b_ref[i]
            moved = acc + beta * g_ref[i]
            new = moved * moved + base * (direction * direction)
        out_ref[i] = acc
        if stage < 3:
            for z in range(DEPTH):
                all_ref[z * ROWS + i] = acc
        return square + new

    square = lax.fori_loop(0, ROWS, body, jnp.zeros((VEC, BLK), F32))
    part_ref[...] = column_sums(square)


def gram_kernel(x_ref, g_ref, gr_ref, part_ref, *refs):
    lefts, out_ref = refs[:NX], refs[NX]
    own = lefts[0]
    total = jnp.zeros((2 * NX * VEC, 4 * VEC), F32)
    for i in range(ROWS):
        left = jnp.concatenate(
            [lefts[k][i] for k in range(NX)] + [lefts[k][ROWS + i] for k in range(NX)], axis=0
        )
        right = jnp.concatenate([own[i], own[ROWS + i], g_ref[i], gr_ref[i]], axis=0)
        total = total + lax.dot_general(
            left,
            right,
            (((1,), (1,)), ((), ())),
            precision=lax.Precision.HIGHEST,
            preferred_element_type=F32,
        )
    both = jnp.concatenate([total[: NX * VEC], total[NX * VEC :]], axis=1)
    for k in range(NX):
        start = pl.multiple_of(((x_ref[0] + NX - k) % NX) * VEC, VEC)
        out_ref[pl.ds(start, VEC), :] = both[k * VEC : (k + 1) * VEC]
    tail = part_ref[...].T[:1, :]
    tail = jnp.concatenate([tail, jnp.zeros((1, BLK - VEC), F32)], axis=1)
    out_ref[NX * VEC :, :] = jnp.broadcast_to(tail, (8, BLK))


def sum_kernel(*refs):
    xs = [ref[...] for ref in refs[:-1]]
    while len(xs) > 1:
        xs = [a + b for a, b in zip(xs[::2], xs[1::2])]
    refs[-1][...] = xs[0]


def add_up(x, *bits):
    every = [x] + [
        lax.ppermute(x, "rows", [(d, d ^ k) for d in range(PEERS)]) for k in bits
    ]
    return pl.pallas_call(
        sum_kernel,
        in_specs=[IN_VMEM] * len(every),
        out_specs=IN_VMEM,
        out_shape=shape(*x.shape),
        compiler_params=params(4),
        name="sum",
    )(*every)


def shards(hblocks, col_index, right_side, center, shifts, filter_weights):
    device = lax.axis_index("rows").astype(jnp.int32)
    my_z, my_p = device // PLANE, device % PLANE
    my = jnp.stack([my_z, my_p])
    own_cols = col_index[:, :NEAR] - device * ROWS
    flat = col_index[:, NEAR:].reshape(-1)
    owner = flat // ROWS
    smaller = (owner[:, None] == owner[None, :]) & (flat[None, :] < flat[:, None])
    slot = (owner // PLANE) * 2 + jnp.any(smaller, axis=1).astype(jnp.int32)
    owner_p = owner % PLANE
    there = ((owner_p // 2 + NY - my_p // 2) % NY) * 2 + (my_p + owner_p) % 2
    back = ((my_p // 2 + NY - owner_p // 2) % NY) * 2 + (my_p + owner_p) % 2
    to_place = (there * SLOTS + slot).reshape(ROWS, FAR)
    from_place = (back * SLOTS + slot).reshape(ROWS, FAR)
    flat_slot = owner_p * SLOTS + slot
    named = flat_slot[None, :] == jnp.arange(PLANE * SLOTS, dtype=jnp.int32)[:, None]
    lists = jnp.max(jnp.where(named, (flat % ROWS)[None, :], 0), axis=1)
    lists_out = jnp.pad(
        lists.astype(F32).reshape(PLANE, 1, SLOTS), ((0, 0), (0, VEC - 1), (0, BLK - SLOTS))
    )

    base_shift = jnp.min(shifts)
    scalars = jnp.stack([center[0], base_shift])
    b = right_side
    h = pltpu.with_memory_space_constraint(hblocks, pltpu.HBM)
    sems = pltpu.SemaphoreType.DMA((ROWS,))
    far_buffer = pltpu.VMEM((ROWS, FAR, BLK, BLK), F32)

    def plane_exchange(xs):
        return [xs[0]] + [lax.ppermute(xs[k], "rows", plane_shift(k)) for k in range(1, PLANE)]

    def depth_exchange(x):
        return lax.all_to_all(
            x, "rows", split_axis=0, concat_axis=0, tiled=True, axis_index_groups=DEPTH_GROUPS
        )

    def far_products(first, v, more):
        return pl.pallas_call(
            functools.partial(far_kernel, first),
            in_specs=[IN_SMEM] * 2 + [IN_VMEM] * 2 + [IN_ANY],
            out_specs=[IN_VMEM] * PLANE,
            out_shape=[shape(SLOTS + (2 if first else 1), VEC, BLK)] * PLANE,
            scratch_shapes=[pltpu.VMEM((PLANE * SLOTS, VEC, BLK), F32), far_buffer, sems],
            compiler_params=params(20),
            name="far",
            cost_estimate=cost(5),
        )(to_place, my, v, more, h)

    def near_products(v):
        return pl.pallas_call(
            near_kernel,
            in_specs=[IN_SMEM, IN_VMEM, IN_ANY],
            out_specs=IN_VMEM,
            out_shape=shape(ROWS, VEC, BLK),
            scratch_shapes=[
                pltpu.VMEM((ROWS, 2 * VEC, BLK), BF16),
                pltpu.VMEM((ROWS, NEAR, BLK, BLK), F32),
                sems,
            ],
            compiler_params=params(12),
            name="near",
            cost_estimate=cost(5),
        )(own_cols, v, h)

    def apply(stage, lists, v, zv, recvs, *more):
        outs = pl.pallas_call(
            middle_kernel,
            in_specs=[IN_SMEM] + [IN_VMEM] * (PLANE + 1),
            out_specs=[IN_VMEM] * (PLANE + 1),
            out_shape=[shape(SLOTS, VEC, BLK)] * PLANE + [shape(DEPTH * UNITS, VEC, BLK)],
            compiler_params=params(12),
            name="middle",
            cost_estimate=cost(2),
        )(lists, zv, *recvs)
        rz = depth_exchange(outs[PLANE])
        fars = plane_exchange(outs[:PLANE])
        w = near_products(v)
        outs = [shape(ROWS * (DEPTH if stage < 3 else 1), VEC, BLK)] + [shape(VEC, BLK)] * 2
        if stage < 3:
            outs.append(shape(ROWS, VEC, BLK))
        if stage == 2:
            outs.append(shape(2 * ROWS, VEC, BLK))
        return pl.pallas_call(
            functools.partial(finish_kernel, stage),
            in_specs=[IN_SMEM] * 2
            + [IN_VMEM] * 3
            + [IN_ANY]
            + [IN_VMEM] * (PLANE + len(more)),
            out_specs=[IN_VMEM] * len(outs),
            out_shape=outs,
            scratch_shapes=[
                pltpu.VMEM((PLANE * SLOTS, 2 * VEC, BLK), BF16),
                far_buffer,
                sems,
            ],
            compiler_params=params(20),
            name="finish",
            cost_estimate=cost(6.5),
        )(from_place, scalars, v, w, rz, h, *fars, *more)

    b_all = jnp.tile(b, (DEPTH, 1, 1))
    zv = depth_exchange(b_all)
    recvs = plane_exchange(far_products(True, b_all, lists_out))
    peer_lists = jnp.stack([r[SLOTS + 1, 0, :SLOTS] for r in recvs]).astype(jnp.int32)
    g0_all, part, rr0, g0 = apply(1, peer_lists, b, zv, recvs)

    zv = depth_exchange(g0_all)
    recvs = plane_exchange(far_products(False, g0, part))
    r1_all, part, moved0, r1, br = apply(2, peer_lists, g0, zv, recvs, b, rr0)

    zv = depth_exchange(r1_all)
    recvs = plane_exchange(far_products(False, r1, part))
    lefts = [br] + [
        lax.ppermute(br, "cols", column_shift(k)) for k in range(1, NX)
    ]
    gr, part, rr1 = apply(3, peer_lists, r1, zv, recvs, b, g0, rr0)

    my_x = lax.axis_index("cols").astype(jnp.int32).reshape(1)
    packed = pl.pallas_call(
        gram_kernel,
        in_specs=[IN_SMEM] + [IN_VMEM] * (3 + NX),
        out_specs=IN_VMEM,
        out_shape=shape(NX * VEC + 8, BLK),
        compiler_params=params(8),
        name="gram",
            cost_estimate=cost(1),
    )(my_x, g0, gr, part, *lefts)
    packed = add_up(packed, 1)
    packed = add_up(packed, 2, 4, 6)
    packed = add_up(packed, PLANE)
    packed = add_up(packed, 2 * PLANE)
    packed = add_up(packed, 4 * PLANE)
    packed, d1 = packed[: NX * VEC], packed[NX * VEC :]

    rr0 = rr0[:, 0]
    d0 = moved0[:, 0] + base_shift * rr0
    rr1 = rr1[:, 0]
    d1 = d1[0, :VEC]
    alpha0 = rr0 / d0
    beta = rr1 / rr0
    alpha1 = rr1 / d1
    delta = (shifts - base_shift)[:, None]
    zeta1 = 1.0 / (1.0 + delta * alpha0)
    zeta2 = zeta1 * alpha0 / (alpha1 * beta * (1.0 - zeta1) + alpha0 * (1.0 + delta * alpha1))
    weights = filter_weights[:, None]
    coef_b = jnp.sum(weights * (alpha0 * zeta1 + alpha1 * beta * zeta1 * zeta2), axis=0)
    coef_r = jnp.sum(weights * (alpha1 * zeta2), axis=0)
    filtered = coef_b[None, :, None] * b + coef_r[None, :, None] * r1
    coefs = jnp.stack([coef_b, coef_r])
    coefs = jnp.stack([coefs] + [lax.ppermute(coefs, "cols", column_shift(k)) for k in range(1, NX)])
    source = (my_x - jnp.arange(NX, dtype=jnp.int32)) % NX
    order = source[:, None] == jnp.arange(NX, dtype=jnp.int32)[None, :]
    all_coef = jnp.sum(jnp.where(order[:, :, None, None], coefs[:, None], 0.0), axis=0)
    left_b = all_coef[:, 0].reshape(-1, 1)
    left_r = all_coef[:, 1].reshape(-1, 1)
    n = VEC
    mixed = left_b * packed[: NX * n, : 4 * n] + left_r * packed[: NX * n, 4 * n :]
    gram_matrix = mixed[:, :n] * coef_b + mixed[:, n : 2 * n] * coef_r
    ritz = mixed[:, 2 * n : 3 * n] * coef_b + mixed[:, 3 * n :] * coef_r
    ritz = ritz + center[0] * gram_matrix
    return filtered, gram_matrix / TOTAL_ROWS, ritz / TOTAL_ROWS


def solution(mesh):
    placed = (P("rows", None, None, None), P("rows", None), P("rows", "cols", None), P(), P(), P())
    return jax.shard_map(
        shards,
        mesh=mesh,
        in_specs=placed,
        out_specs=(P("rows", "cols", None), P(None, "cols"), P(None, "cols")),
        check_vma=False,
    )
```

```python
import functools

import jax
import jax.numpy as jnp
from jax import lax
from jax.experimental import pallas as pl
from jax.experimental.pallas import tpu as pltpu
from jax.sharding import PartitionSpec as P

F32 = jnp.float32
BF16 = jnp.bfloat16
ROWS = 8
NEAR = 8
FAR = 16
VEC = 16
BLK = 128
PEERS = 64
PLANE = 8
DEPTH = 8
NY = 4
NX = 4
SLOTS = 16
UNITS = ROWS + 1
TOTAL_ROWS = 65536.0

DEPTH_GROUPS = [[z * PLANE + p for z in range(DEPTH)] for p in range(PLANE)]

IN_VMEM = pl.BlockSpec(memory_space=pltpu.VMEM)
IN_SMEM = pl.BlockSpec(memory_space=pltpu.SMEM)
IN_ANY = pl.BlockSpec(memory_space=pl.ANY)


def params(mib):
    return pltpu.CompilerParams(vmem_limit_bytes=mib * 1024 * 1024)


def cost(us):
    return pl.CostEstimate(flops=int(us * 1e9), bytes_accessed=int(us * 3.2e6), transcendentals=0)


def shape(*dims):
    return jax.ShapeDtypeStruct(dims, F32)


def peer_number(k, p):
    return ((p // 2 + k // 2) % NY) * 2 + (p % 2 + k % 2) % 2


def plane_shift(k):
    return [
        (z * PLANE + p, z * PLANE + peer_number(k, p)) for z in range(DEPTH) for p in range(PLANE)
    ]


def column_shift(k):
    return [(x, (x + k) % NX) for x in range(NX)]


def two_parts(x):
    high = x.astype(BF16)
    return high, (x - high.astype(F32)).astype(BF16)


def stacked(x):
    return jnp.concatenate(two_parts(x), axis=0)


def fold(d):
    return (d[:VEC, :BLK] + d[VEC:, BLK:]) + d[VEC:, :BLK] + d[:VEC, BLK:]


def times_block(vs, high, low):
    return fold(jnp.dot(vs, jnp.concatenate([high, low], axis=1), preferred_element_type=F32))


def times_blocks_t(ns, blocks):
    weights = jnp.concatenate(
        [jnp.concatenate([b[part] for b in blocks], axis=1) for part in range(2)], axis=0
    )
    return fold(
        lax.dot_general(
            jnp.concatenate(ns, axis=1),
            weights,
            (((1,), (1,)), ((), ())),
            preferred_element_type=F32,
        )
    )


def column_sums(x):
    return jnp.broadcast_to(jnp.sum(x, axis=1, keepdims=True), (VEC, BLK))


def start_copies(h_ref, first, buffer, sems):
    count = buffer.shape[1]
    for i in range(ROWS):
        pltpu.make_async_copy(
            h_ref.at[i, pl.ds(first, count)], buffer.at[i], sems.at[i]
        ).start()


def wait_copy(h_ref, first, buffer, sems, i):
    count = buffer.shape[1]
    pltpu.make_async_copy(h_ref.at[i, pl.ds(first, count)], buffer.at[i], sems.at[i]).wait()


def far_kernel(first, place_ref, my_ref, v_ref, more_ref, h_ref, *refs):
    outs, (acc_ref, buffer, sems) = refs[:PLANE], refs[PLANE:]
    start_copies(h_ref, NEAR, buffer, sems)
    acc_ref[...] = jnp.zeros_like(acc_ref)
    if first:
        part = jnp.zeros((VEC, BLK), F32)
        for i in range(ROWS):
            part = part + v_ref[i] * v_ref[i]
        part = column_sums(part)
        for k in range(PLANE):
            outs[k][SLOTS + 1] = more_ref[peer_number(k, my_ref[1])]
    else:
        part = more_ref[...]

    def body(i, carry):
        vs = stacked(v_ref[i])
        wait_copy(h_ref, NEAR, buffer, sems, i)
        for k in range(FAR):
            acc_ref[place_ref[i, k]] += times_block(vs, *two_parts(buffer[i, k]))
        return carry

    lax.fori_loop(0, ROWS, body, 0)
    for k in range(PLANE):
        outs[k][:SLOTS] = acc_ref[k * SLOTS : (k + 1) * SLOTS]
        outs[k][SLOTS] = part


def near_kernel(own_ref, v_ref, h_ref, w_ref, parts, buffer, sems):
    start_copies(h_ref, 0, buffer, sems)
    for i in range(ROWS):
        parts[i] = stacked(v_ref[i])
    w_ref[...] = jnp.zeros_like(w_ref)

    def body(i, carry):
        vs = parts[i]
        acc = jnp.zeros((VEC, BLK), F32)
        wait_copy(h_ref, 0, buffer, sems, i)
        for k in range(0, NEAR, 2):
            blocks = [two_parts(buffer[i, q]) for q in (k, k + 1)]
            acc = acc + times_blocks_t(
                [parts[own_ref[i, k]], parts[own_ref[i, k + 1]]], blocks
            )
            for q in range(2):
                w_ref[own_ref[i, k + q]] += times_block(vs, *blocks[q])
        w_ref[i] += acc
        return carry

    lax.fori_loop(0, ROWS, body, 0)


def middle_kernel(list_ref, zv_ref, *refs):
    recvs, outs, zacc_ref = refs[:PLANE], refs[-PLANE - 1 : -1], refs[-1]
    for k in range(PLANE):
        back = ((NY - k // 2) % NY) * 2 + k % 2
        for s in range(SLOTS):
            outs[k][s] = zv_ref[(s // 2) * ROWS + list_ref[back, s]]
    zacc_ref[...] = jnp.zeros_like(zacc_ref)
    part = recvs[0][SLOTS]
    for k in range(1, PLANE):
        part = part + recvs[k][SLOTS]
    for z in range(DEPTH):
        zacc_ref[z * UNITS + ROWS] = part
    for s in range(SLOTS):
        for k in range(PLANE):
            zacc_ref[(s // 2) * UNITS + list_ref[k, s]] += recvs[k][s]


def far_rows(place_ref, v_ref, acc_ref, buffer, outs, units):
    acc_ref[...] = jnp.zeros_like(acc_ref)

    def body(i, carry):
        vs = stacked(v_ref[i])
        for k in range(FAR):
            acc_ref[place_ref[i, k]] += times_block(vs, *two_parts(buffer[i, k]))
        return carry

    lax.fori_loop(0, ROWS, body, 0)
    for k in range(PLANE):
        outs[k][:SLOTS] = acc_ref[k * SLOTS : (k + 1) * SLOTS]


def finish_kernel(stage, place_ref, to_ref, scal_ref, v_ref, w_ref, rz_ref, h_ref, *refs):
    fars, refs = refs[:PLANE], refs[PLANE:]
    refs, (parts, buffer, acc_ref, sems) = refs[:-4], refs[-4:]
    if stage < 3:
        refs, sends = refs[:-PLANE], refs[-PLANE:]
    start_copies(h_ref, NEAR, buffer, sems)
    center, base = scal_ref[0], scal_ref[1]
    total = rz_ref[ROWS]
    for z in range(1, DEPTH):
        total = total + rz_ref[z * UNITS + ROWS]
    for k in range(PLANE):
        for s in range(SLOTS):
            parts[k * SLOTS + s] = stacked(fars[k][s])
    if stage == 1:
        all_ref, part_ref, tot_ref, out_ref = refs
    elif stage == 2:
        b_ref, rr_ref, all_ref, part_ref, tot_ref, out_ref, br_ref = refs
        rr = rr_ref[...]
        alpha = rr / (total + base * rr)
    else:
        b_ref, g_ref, rr_ref, out_ref, part_ref, tot_ref = refs
        beta = total / rr_ref[...]
    tot_ref[...] = total

    def body(i, square):
        acc = w_ref[i] - center * v_ref[i]
        for z in range(DEPTH):
            acc = acc + rz_ref[z * UNITS + i]
        wait_copy(h_ref, NEAR, buffer, sems, i)
        for k in range(0, FAR, 4):
            ks = range(k, k + 4)
            acc = acc + times_blocks_t(
                [parts[place_ref[i, q]] for q in ks], [two_parts(buffer[i, q]) for q in ks]
            )
        if stage == 1:
            new = acc * acc
        elif stage == 2:
            acc = b_ref[i] - alpha * (acc + base * b_ref[i])
            br_ref[i] = b_ref[i]
            br_ref[ROWS + i] = acc
            new = acc * acc
        else:
            direction = v_ref[i] + beta * b_ref[i]
            moved = acc + beta * g_ref[i]
            new = moved * moved + base * (direction * direction)
        out_ref[i] = acc
        if stage < 3:
            for z in range(DEPTH):
                all_ref[z * ROWS + i] = acc
        return square + new

    square = lax.fori_loop(0, ROWS, body, jnp.zeros((VEC, BLK), F32))
    part = column_sums(square)
    part_ref[...] = part
    if stage < 3:
        far_rows(to_ref, out_ref, acc_ref, buffer, sends, SLOTS + 1)
        for k in range(PLANE):
            sends[k][SLOTS] = part


def gram_kernel(x_ref, g_ref, gr_ref, part_ref, *refs):
    lefts, out_ref = refs[:NX], refs[NX]
    own = lefts[0]
    total = jnp.zeros((2 * NX * VEC, 4 * VEC), F32)
    for i in range(ROWS):
        left = jnp.concatenate(
            [lefts[k][i] for k in range(NX)] + [lefts[k][ROWS + i] for k in range(NX)], axis=0
        )
        right = jnp.concatenate([own[i], own[ROWS + i], g_ref[i], gr_ref[i]], axis=0)
        total = total + lax.dot_general(
            left,
            right,
            (((1,), (1,)), ((), ())),
            precision=lax.Precision.HIGHEST,
            preferred_element_type=F32,
        )
    both = jnp.concatenate([total[: NX * VEC], total[NX * VEC :]], axis=1)
    for k in range(NX):
        start = pl.multiple_of(((x_ref[0] + NX - k) % NX) * VEC, VEC)
        out_ref[pl.ds(start, VEC), :] = both[k * VEC : (k + 1) * VEC]
    tail = part_ref[...].T[:1, :]
    tail = jnp.concatenate([tail, jnp.zeros((1, BLK - VEC), F32)], axis=1)
    out_ref[NX * VEC :, :] = jnp.broadcast_to(tail, (8, BLK))


def sum_kernel(*refs):
    xs = [ref[...] for ref in refs[:-1]]
    while len(xs) > 1:
        xs = [a + b for a, b in zip(xs[::2], xs[1::2])]
    refs[-1][...] = xs[0]


def add_up(x, *bits):
    every = [x] + [
        lax.ppermute(x, "rows", [(d, d ^ k) for d in range(PEERS)]) for k in bits
    ]
    return pl.pallas_call(
        sum_kernel,
        in_specs=[IN_VMEM] * len(every),
        out_specs=IN_VMEM,
        out_shape=shape(*x.shape),
        compiler_params=params(4),
        name="sum",
    )(*every)


def shards(hblocks, col_index, right_side, center, shifts, filter_weights):
    device = lax.axis_index("rows").astype(jnp.int32)
    my_z, my_p = device // PLANE, device % PLANE
    my = jnp.stack([my_z, my_p])
    own_cols = col_index[:, :NEAR] - device * ROWS
    flat = col_index[:, NEAR:].reshape(-1)
    owner = flat // ROWS
    smaller = (owner[:, None] == owner[None, :]) & (flat[None, :] < flat[:, None])
    slot = (owner // PLANE) * 2 + jnp.any(smaller, axis=1).astype(jnp.int32)
    owner_p = owner % PLANE
    there = ((owner_p // 2 + NY - my_p // 2) % NY) * 2 + (my_p + owner_p) % 2
    back = ((my_p // 2 + NY - owner_p // 2) % NY) * 2 + (my_p + owner_p) % 2
    to_place = (there * SLOTS + slot).reshape(ROWS, FAR)
    from_place = (back * SLOTS + slot).reshape(ROWS, FAR)
    flat_slot = owner_p * SLOTS + slot
    named = flat_slot[None, :] == jnp.arange(PLANE * SLOTS, dtype=jnp.int32)[:, None]
    lists = jnp.max(jnp.where(named, (flat % ROWS)[None, :], 0), axis=1)
    lists_out = jnp.pad(
        lists.astype(F32).reshape(PLANE, 1, SLOTS), ((0, 0), (0, VEC - 1), (0, BLK - SLOTS))
    )

    base_shift = jnp.min(shifts)
    scalars = jnp.stack([center[0], base_shift])
    b = right_side
    h = pltpu.with_memory_space_constraint(hblocks, pltpu.HBM)
    sems = pltpu.SemaphoreType.DMA((ROWS,))
    far_buffer = pltpu.VMEM((ROWS, FAR, BLK, BLK), F32)

    def plane_exchange(xs):
        return [xs[0]] + [lax.ppermute(xs[k], "rows", plane_shift(k)) for k in range(1, PLANE)]

    def depth_exchange(x):
        return lax.all_to_all(
            x, "rows", split_axis=0, concat_axis=0, tiled=True, axis_index_groups=DEPTH_GROUPS
        )

    def far_products(first, v, more):
        return pl.pallas_call(
            functools.partial(far_kernel, first),
            in_specs=[IN_SMEM] * 2 + [IN_VMEM] * 2 + [IN_ANY],
            out_specs=[IN_VMEM] * PLANE,
            out_shape=[shape(SLOTS + (2 if first else 1), VEC, BLK)] * PLANE,
            scratch_shapes=[pltpu.VMEM((PLANE * SLOTS, VEC, BLK), F32), far_buffer, sems],
            compiler_params=params(20),
            name="far",
            cost_estimate=cost(5),
        )(to_place, my, v, more, h)

    def near_products(v):
        return pl.pallas_call(
            near_kernel,
            in_specs=[IN_SMEM, IN_VMEM, IN_ANY],
            out_specs=IN_VMEM,
            out_shape=shape(ROWS, VEC, BLK),
            scratch_shapes=[
                pltpu.VMEM((ROWS, 2 * VEC, BLK), BF16),
                pltpu.VMEM((ROWS, NEAR, BLK, BLK), F32),
                sems,
            ],
            compiler_params=params(12),
            name="near",
            cost_estimate=cost(5),
        )(own_cols, v, h)

    def apply(stage, lists, v, zv, recvs, *more):
        outs = pl.pallas_call(
            middle_kernel,
            in_specs=[IN_SMEM] + [IN_VMEM] * (PLANE + 1),
            out_specs=[IN_VMEM] * (PLANE + 1),
            out_shape=[shape(SLOTS, VEC, BLK)] * PLANE + [shape(DEPTH * UNITS, VEC, BLK)],
            compiler_params=params(12),
            name="middle",
            cost_estimate=cost(2),
        )(lists, zv, *recvs)
        rz = depth_exchange(outs[PLANE])
        fars = plane_exchange(outs[:PLANE])
        w = near_products(v)
        outs = [shape(ROWS * (DEPTH if stage < 3 else 1), VEC, BLK)] + [shape(VEC, BLK)] * 2
        if stage < 3:
            outs.append(shape(ROWS, VEC, BLK))
        if stage == 2:
            outs.append(shape(2 * ROWS, VEC, BLK))
        if stage < 3:
            outs += [shape(SLOTS + 1, VEC, BLK)] * PLANE
        return pl.pallas_call(
            functools.partial(finish_kernel, stage),
            in_specs=[IN_SMEM] * 3
            + [IN_VMEM] * 3
            + [IN_ANY]
            + [IN_VMEM] * (PLANE + len(more)),
            out_specs=[IN_VMEM] * len(outs),
            out_shape=outs,
            scratch_shapes=[
                pltpu.VMEM((PLANE * SLOTS, 2 * VEC, BLK), BF16),
                far_buffer,
                pltpu.VMEM((PLANE * SLOTS, VEC, BLK), F32),
                sems,
            ],
            compiler_params=params(20),
            name="finish",
            cost_estimate=cost(6.5),
        )(from_place, to_place, scalars, v, w, rz, h, *fars, *more)

    b_all = jnp.tile(b, (DEPTH, 1, 1))
    zv = depth_exchange(b_all)
    recvs = plane_exchange(far_products(True, b_all, lists_out))
    peer_lists = jnp.stack([r[SLOTS + 1, 0, :SLOTS] for r in recvs]).astype(jnp.int32)
    g0_all, part, rr0, g0, *sends = apply(1, peer_lists, b, zv, recvs)

    zv = depth_exchange(g0_all)
    recvs = plane_exchange(sends)
    r1_all, part, moved0, r1, br, *sends = apply(2, peer_lists, g0, zv, recvs, b, rr0)

    zv = depth_exchange(r1_all)
    recvs = plane_exchange(sends)
    lefts = [br] + [
        lax.ppermute(br, "cols", column_shift(k)) for k in range(1, NX)
    ]
    gr, part, rr1 = apply(3, peer_lists, r1, zv, recvs, b, g0, rr0)

    my_x = lax.axis_index("cols").astype(jnp.int32).reshape(1)
    packed = pl.pallas_call(
        gram_kernel,
        in_specs=[IN_SMEM] + [IN_VMEM] * (3 + NX),
        out_specs=IN_VMEM,
        out_shape=shape(NX * VEC + 8, BLK),
        compiler_params=params(8),
        name="gram",
            cost_estimate=cost(1),
    )(my_x, g0, gr, part, *lefts)
    packed = add_up(packed, 1)
    packed = add_up(packed, 2, 4, 6)
    packed = add_up(packed, PLANE)
    packed = add_up(packed, 2 * PLANE)
    packed = add_up(packed, 4 * PLANE)
    packed, d1 = packed[: NX * VEC], packed[NX * VEC :]

    rr0 = rr0[:, 0]
    d0 = moved0[:, 0] + base_shift * rr0
    rr1 = rr1[:, 0]
    d1 = d1[0, :VEC]
    alpha0 = rr0 / d0
    beta = rr1 / rr0
    alpha1 = rr1 / d1
    delta = (shifts - base_shift)[:, None]
    zeta1 = 1.0 / (1.0 + delta * alpha0)
    zeta2 = zeta1 * alpha0 / (alpha1 * beta * (1.0 - zeta1) + alpha0 * (1.0 + delta * alpha1))
    weights = filter_weights[:, None]
    coef_b = jnp.sum(weights * (alpha0 * zeta1 + alpha1 * beta * zeta1 * zeta2), axis=0)
    coef_r = jnp.sum(weights * (alpha1 * zeta2), axis=0)
    filtered = coef_b[None, :, None] * b + coef_r[None, :, None] * r1
    coefs = jnp.stack([coef_b, coef_r])
    coefs = jnp.stack([coefs] + [lax.ppermute(coefs, "cols", column_shift(k)) for k in range(1, NX)])
    source = (my_x - jnp.arange(NX, dtype=jnp.int32)) % NX
    order = source[:, None] == jnp.arange(NX, dtype=jnp.int32)[None, :]
    all_coef = jnp.sum(jnp.where(order[:, :, None, None], coefs[:, None], 0.0), axis=0)
    left_b = all_coef[:, 0].reshape(-1, 1)
    left_r = all_coef[:, 1].reshape(-1, 1)
    n = VEC
    mixed = left_b * packed[: NX * n, : 4 * n] + left_r * packed[: NX * n, 4 * n :]
    gram_matrix = mixed[:, :n] * coef_b + mixed[:, n : 2 * n] * coef_r
    ritz = mixed[:, 2 * n : 3 * n] * coef_b + mixed[:, 3 * n :] * coef_r
    ritz = ritz + center[0] * gram_matrix
    return filtered, gram_matrix / TOTAL_ROWS, ritz / TOTAL_ROWS


def solution(mesh):
    placed = (P("rows", None, None, None), P("rows", None), P("rows", "cols", None), P(), P(), P())
    return jax.shard_map(
        shards,
        mesh=mesh,
        in_specs=placed,
        out_specs=(P("rows", "cols", None), P(None, "cols"), P(None, "cols")),
        check_vma=False,
    )
```
